32 devices in a mesh: groups: 2 (over y), gx: 4 (over z), gy: 4 (over x, core).
Axes of the slice: x: 2, y: 2, z: 4, core: 2. Of those that a mesh axis runs over, the one named last changes fastest.
Arguments:
- mean_field: float32 [3, 8, 8, 512], P(None, ('groups', 'gx'), None, 'gy'), parts along dimension 1, may hold values from -6 to 6
- modes: float32 [32, 3, 8, 8, 512], P(None, None, ('groups', 'gx'), None, 'gy'), parts along dimension 2, may hold values from -6 to 6
- samples: float32 [32, 32768], P(None, ('groups', 'gx', 'gy')), parts along dimension 1, may hold values from -41 to 41, as said below
Outputs:
- mean_rate: float32 [3, 8, 8, 512], P(None, ('groups', 'gx'), None, 'gy'), parts along dimension 1
- modes_tendency: float32 [32, 3, 8, 8, 512], P(None, None, ('groups', 'gx'), None, 'gy'), parts along dimension 2
- sample_rate: float32 [32, 32768], P(None, ('groups', 'gx', 'gy')), parts along dimension 1
The draws below stay inside these ranges and needn't reach their ends.
There are 2 independent parts, one for each index of `groups`. The reference program is written for one: setup_inputs(seed, part) draws one part's arguments, and reference() takes and returns one part's arrays. A program takes and returns all parts, laid end to end along the dimension named above; each array names one. Nothing has to cross between parts.
Inputs may be any that keep to these rules, and one draw needn't show every extreme that they name: `samples`: samples of different modes have different spreads and are correlated; their distribution is skewed.
All inputs are finite; a program needn't handle non-finite values.
Results may differ from the reference program's by a relative error of at most 0.00012.
Values sent between devices are 32-bit elements; how exact they have to be, the bound alone decides.
A program may use at most 128 MiB of HBM per device.

```python
import math
import jax
import jax.numpy as jnp
from jax import lax

K = 32
NZ = 8
NX = 4
NY = 512
SAMPLES = 16384


def draw_samples(key, part):
    key = jax.random.fold_in(key, 7)
    keys = jax.random.split(key, 4)
    spread = jnp.exp(jax.random.uniform(keys[0], (K, 1), minval=jnp.log(0.3), maxval=jnp.log(3.0)))
    first = jnp.clip(jax.random.normal(keys[1], (K, SAMPLES)), -4.0, 4.0)
    second = jnp.clip(jax.random.normal(keys[2], (K, SAMPLES)), -4.0, 4.0)
    common = jnp.clip(jax.random.normal(keys[3], (1, SAMPLES)), -4.0, 4.0)
    value_entries = spread * (first + 0.5 * (second * second - 1.0) + 0.5 * common)
    return value_entries.astype(jnp.float32)


def block_levels(own_key, extent, cuts, smallest, largest):
    factor_of, own = 1.0, jax.random.fold_in(own_key, 6)
    for dim, parts in cuts:
        heights = jnp.exp(jax.random.uniform(jax.random.fold_in(own, dim), (parts,), jnp.float32, smallest / len(cuts), largest / len(cuts)))
        factor_of = factor_of * jnp.repeat(heights, extent[dim] // parts).reshape([-1 if axis == dim else 1 for axis in range(len(extent))])
    return factor_of


def bell_draw(key, extent, scale, reach, cuts=(), dtype=jnp.bfloat16):
    values = scale * jax.random.normal(key, extent, jnp.float32)
    if cuts:
        values = values * block_levels(key, extent, cuts, -0.22, 0.18)
    return jnp.clip(values, -reach, reach).astype(dtype)


def setup_inputs(seed: int = 0, part: int = 0) -> dict:
    arg_keys = jax.random.split(jax.random.key(seed), 4)
    own_keys = jax.random.split(jax.random.fold_in(arg_keys[3], part), 4)
    mean_field = bell_draw(own_keys[0], (3, NX, NZ, NY), 1.0, 6.0, ((1, 4), (3, 4)), jnp.float32)
    modes = bell_draw(own_keys[1], (K, 3, NX, NZ, NY), 1.0, 6.0, ((2, 4), (4, 4)), jnp.float32)
    samples = draw_samples(jax.random.fold_in(jax.random.fold_in(arg_keys[3], part), 71), part)
    return dict(mean_field=mean_field, modes=modes, samples=samples)


top_degree = lax.Precision.HIGHEST
viscosity = 0.2

def derivatives(fields):
    widened = jnp.pad(fields, ((0, 0), (0, 0), (0, 0), (1, 1), (0, 0)))
    centre = widened[:, :, :, 1:-1, :]
    x_plus = jnp.roll(centre, -1, axis=2)
    x_minus = jnp.roll(centre, 1, axis=2)
    y_plus = jnp.roll(centre, -1, axis=4)
    y_minus = jnp.roll(centre, 1, axis=4)
    z_plus = widened[:, :, :, 2:, :]
    z_minus = widened[:, :, :, :-2, :]
    gradient = jnp.stack([(x_plus - x_minus) * 0.5, (y_plus - y_minus) * 0.5, (z_plus - z_minus) * 0.5], axis=2)
    laplace = x_plus + x_minus + y_plus + y_minus + z_plus + z_minus - 6.0 * centre
    return (centre, gradient, laplace)

def into_blocks(array, width):
    shape = array.shape
    pieces = shape[-1] // width
    return jnp.moveaxis(array.reshape(shape[:-1] + (pieces, width)), -2, 0)

def triple_products(basis_matrix, basis_slopes, width):
    number = basis_matrix.shape[0]

    def step_forward(summed, pieces):
        value_entries, slope_arrays = pieces
        weighted_terms = jnp.einsum('rsf,nsbf->rnbf', value_entries, slope_arrays, precision=top_degree)
        return (summed + jnp.einsum('kdc,ildc->ikl', value_entries, weighted_terms, precision=top_degree), None)
    summed, _ = lax.scan(step_forward, jnp.zeros((number, number, number), jnp.float32), (into_blocks(basis_matrix, width), into_blocks(basis_slopes, width)))
    return summed

def mode_advection(folded, basis_matrix, basis_slopes, width):
    number = basis_matrix.shape[0]

    def step_forward(carried_over, pieces):
        value_entries, slope_arrays = pieces
        velocity_field = jnp.einsum('ikl,kdc->ildc', folded, value_entries, precision=top_degree)
        return (carried_over, jnp.einsum('nyfu,ytfu->ntu', velocity_field, slope_arrays, precision=top_degree))
    _, stacked = lax.scan(step_forward, jnp.zeros((), jnp.float32), (into_blocks(basis_matrix, width), into_blocks(basis_slopes, width)))
    return jnp.moveaxis(stacked, 0, 2).reshape(number, 3, -1)

def third_moment(value_entries, width):
    number = value_entries.shape[0]

    def step_forward(summed, piece):
        pairs = (piece[:, None, :] * piece[None, :, :]).reshape(number * number, -1)
        return (summed + jnp.dot(piece.astype(jnp.float32), pairs.T.astype(jnp.float32), precision=top_degree, preferred_element_type=jnp.float32), None)
    summed, _ = lax.scan(step_forward, jnp.zeros((number, number * number), jnp.float32), into_blocks(value_entries, width))
    return summed.reshape(number, number, number)

def sample_response(centred, linear_projection, triple_proj, covariance, width):
    number = centred.shape[0]
    flat_proj = triple_proj.reshape(number, number * number)
    offset = jnp.sum(triple_proj * covariance[None], axis=(1, 2))

    def step_forward(carried_over, piece):
        pairs = (piece[:, None, :] * piece[None, :, :]).reshape(number * number, -1)
        result = jnp.dot(linear_projection.T.astype(jnp.float32), piece.astype(jnp.float32), precision=top_degree, preferred_element_type=jnp.float32)
        result = result - jnp.dot(flat_proj.astype(jnp.float32), pairs.astype(jnp.float32), precision=top_degree, preferred_element_type=jnp.float32)
        return (carried_over, result + offset[:, None])
    _, stacked = lax.scan(step_forward, jnp.zeros((), jnp.float32), into_blocks(centred, width))
    return jnp.moveaxis(stacked, 0, 1).reshape(number, -1)

def reference(mean_field, modes, samples):
    number = modes.shape[0]
    fields = jnp.concatenate([mean_field[None], modes], axis=0)
    centre, gradient, laplace = derivatives(fields)
    grid_samples = centre.shape[2] * centre.shape[3] * centre.shape[4]
    basis_matrix = centre[1:].reshape(number, 3, grid_samples)
    mean_flat = centre[0].reshape(3, grid_samples)
    basis_slopes = gradient[1:].reshape(number, 3, 3, grid_samples)
    mean_grad = gradient[0].reshape(3, 3, grid_samples)
    modes_lap = laplace[1:].reshape(number, 3, grid_samples)
    mean_lap = laplace[0].reshape(3, grid_samples)
    linear_term = -jnp.einsum('dc,kedc->kec', mean_flat, basis_slopes, precision=top_degree) - jnp.einsum('kdc,edc->kec', basis_matrix, mean_grad, precision=top_degree) + viscosity * modes_lap
    cell_width = math.gcd(grid_samples, 4096)
    linear_projection = jnp.einsum('pxa,qxa->pq', linear_term, basis_matrix, precision=top_degree) / grid_samples
    triple_proj = triple_products(basis_matrix, basis_slopes, cell_width) / grid_samples
    sample_count = samples.shape[1]
    sample_width = math.gcd(sample_count, 4096)
    average = jnp.sum(samples, axis=1) / sample_count
    centred = samples - average[:, None]
    covariance = jnp.dot(centred.astype(jnp.float32), centred.T.astype(jnp.float32), precision=top_degree, preferred_element_type=jnp.float32) / sample_count
    skewness = third_moment(centred, sample_width) / sample_count
    factor = jnp.linalg.cholesky(covariance)
    folded = jax.scipy.linalg.cho_solve((factor, True), skewness.reshape(number, number * number)).reshape(number, number, number)
    growth_rate_grid = linear_term - mode_advection(folded, basis_matrix, basis_slopes, cell_width)
    perturbation_heading = jnp.einsum('iyn,ayn->ia', growth_rate_grid, basis_matrix, precision=top_degree) / grid_samples
    modes_tendency = growth_rate_grid - jnp.einsum('yn,nbv->ybv', perturbation_heading, basis_matrix, precision=top_degree)
    mixed_grad = jnp.einsum('kl,ledc->kedc', covariance, basis_slopes, precision=top_degree)
    mean_rate = -jnp.einsum('dc,edc->ec', mean_flat, mean_grad, precision=top_degree) + viscosity * mean_lap - jnp.einsum('kdc,kedc->ec', basis_matrix, mixed_grad, precision=top_degree)
    sample_rate = sample_response(centred, linear_projection, triple_proj, covariance, sample_width)
    return (mean_rate.reshape(mean_field.shape), modes_tendency.reshape(modes.shape), sample_rate)
```

```python
import functools

import jax
import jax.numpy as jnp
from jax import lax
from jax.experimental import pallas as pl
from jax.experimental.pallas import tpu as pltpu
from jax.sharding import PartitionSpec as P

MESH = pl.DeviceIdType.MESH
top_degree = lax.Precision.HIGHEST
viscosity = 0.2
f32, bf16 = jnp.float32, jnp.bfloat16

K = 32
HALF = 16
NZ = 8
LANES = 128
CELLS = NZ * LANES
PAIRS = HALF * HALF + HALF * K
WIDE = PAIRS + LANES
ROWS = 40


def split(x):
    hi = x.astype(bf16)
    return hi, (x - hi.astype(f32)).astype(bf16)


def dot(a, b, precision=None):
    return lax.dot_general(
        a, b, (((1,), (0,)), ((), ())), precision=precision, preferred_element_type=f32
    )


def dot_nt(a, b, precision=None):
    return lax.dot_general(
        a, b, (((1,), (1,)), ((), ())), precision=precision, preferred_element_type=f32
    )


def inverse(matrix):
    lane = lax.broadcasted_iota(jnp.int32, (K, LANES), 1)
    row = lax.broadcasted_iota(jnp.int32, (K, LANES), 0)
    m = jnp.where(lane < K, matrix, jnp.where(lane == row + K, 1.0, 0.0))
    for k in range(K):
        pivot_row = m[k : k + 1, :] / m[k : k + 1, k : k + 1]
        m = jnp.where(row == k, pivot_row, m - m[:, k : k + 1] * pivot_row)
    return m[:, K : 2 * K]


def kernel(
    gx,
    gy,
    mean_ref,
    modes_ref,
    samples_ref,
    mean_out,
    modes_out,
    samples_out,
    xm,
    xp,
    f,
    g,
    lap,
    lin,
    mt,
    bh,
    bl,
    ph,
    plo,
    centred,
    coef,
    avg_own,
    avg_y,
    avg_mid,
    avg_x,
    edge_send,
    edge_recv,
    sb,
    sr1,
    s1,
    sr2,
    sfull,
    tb,
    tr1,
    t1,
    tr2,
    tfull,
    halo_send,
    halo_recv,
    edge_ss,
    edge_rs,
    ay_ss,
    ay_rs,
    ax_ss,
    ax_rs,
    s_ss,
    s_rs,
    sx_ss,
    sx_rs,
    sg_ss,
    sg_rs,
    t_ss,
    t_rs,
    tx_ss,
    tx_rs,
    tg_ss,
    tg_rs,
):
    ix, iy = lax.axis_index("gx"), lax.axis_index("gy")
    members = gx * gy
    sample_total = samples_ref.shape[1] * members
    total_cells = CELLS * members

    barrier = pltpu.get_barrier_semaphore()
    for off in range(1, gx):
        pl.semaphore_signal(
            barrier, inc=1, device_id={"gx": lax.rem(ix + off, gx)}, device_id_type=MESH
        )
    for off in range(1, gy):
        pl.semaphore_signal(
            barrier, inc=1, device_id={"gy": lax.rem(iy + off, gy)}, device_id_type=MESH
        )
    pl.semaphore_wait(barrier, gx + gy - 2)

    def send(src, dst, ss, rs, axis, target):
        copy = pltpu.make_async_remote_copy(
            src_ref=src,
            dst_ref=dst,
            send_sem=ss,
            recv_sem=rs,
            device_id={axis: target},
            device_id_type=MESH,
        )
        copy.start()
        return copy

    x_next, x_prev = lax.rem(ix + 1, gx), lax.rem(ix + gx - 1, gx)
    y_next, y_prev = lax.rem(iy + 1, gy), lax.rem(iy + gy - 1, gy)

    part = samples_ref[:, 0:LANES]
    for z in range(1, samples_ref.shape[1] // LANES):
        part = part + samples_ref[:, z * LANES : (z + 1) * LANES]
    avg_own[...] = part

    def spread(src, slots, ss, rs, axis, index, count):
        return [
            send(src, slots.at[off], ss.at[off], rs.at[off], axis, lax.rem(index + off, count))
            for off in range(1, count)
        ]

    avg_copies = spread(avg_own, avg_y, ay_ss, ay_rs, "gy", iy, gy)

    halo = []
    halo.append(send(mean_ref, xm.at[768:792], halo_send.at[0], halo_recv.at[0], "gx", x_next))
    halo.append(send(mean_ref, xp.at[768:792], halo_send.at[1], halo_recv.at[1], "gx", x_prev))
    for c in range(2):
        rows = slice(c * 384, (c + 1) * 384)
        s = 2 + 2 * c
        halo.append(
            send(modes_ref.at[rows], xm.at[rows], halo_send.at[s], halo_recv.at[s], "gx", x_next)
        )
        halo.append(
            send(
                modes_ref.at[rows],
                xp.at[rows],
                halo_send.at[s + 1],
                halo_recv.at[s + 1],
                "gx",
                x_prev,
            )
        )

    lane = lax.broadcasted_iota(jnp.int32, (ROWS, LANES), 1)
    to_next = jnp.zeros((ROWS, LANES), f32)
    to_prev = jnp.zeros((ROWS, LANES), f32)
    for e in range(3):
        for z in range(NZ):
            j = e * NZ + z
            cols = slice(z * LANES, (z + 1) * LANES)
            f[e, 0:K, cols] = modes_ref[pl.ds(j, K, stride=24), :]
            f[e, K:ROWS, cols] = jnp.broadcast_to(mean_ref[j : j + 1, :], (ROWS - K, LANES))
            piece = f[e, :, cols]
            to_next = jnp.where(lane == j, pltpu.roll(piece, j + 1, 1), to_next)
            to_prev = jnp.where(lane == j, pltpu.roll(piece, j, 1) if j else piece, to_prev)
    edge_send[0] = to_next
    edge_send[1] = to_prev
    edges = [
        send(edge_send.at[0], edge_recv.at[0], edge_ss.at[0], edge_rs.at[0], "gy", y_next),
        send(edge_send.at[1], edge_recv.at[1], edge_ss.at[1], edge_rs.at[1], "gy", y_prev),
    ]
    for e in range(3):
        hi, lo = split(f[e, 0:K, :])
        mt[e, 0:K, :] = hi
        mt[e, K : 2 * K, :] = lo

    for copy in avg_copies:
        copy.wait()
    total = avg_own[...]
    for off in range(1, gy):
        total = total + avg_y[off]
    avg_mid[...] = total
    avg_copies = spread(avg_mid, avg_x, ax_ss, ax_rs, "gx", ix, gx)

    for copy in edges:
        copy.wait()
    for e in range(3):
        for z in range(NZ):
            j = e * NZ + z
            cols = slice(z * LANES, (z + 1) * LANES)
            piece = f[e, :, cols]
            before = jnp.where(
                lane == 0, pltpu.roll(edge_recv[0], LANES - j, 1) if j else edge_recv[0],
                pltpu.roll(piece, 1, 1),
            )
            after = jnp.where(
                lane == LANES - 1, pltpu.roll(edge_recv[1], LANES - 1 - j, 1),
                pltpu.roll(piece, LANES - 1, 1),
            )
            zero = jnp.zeros_like(piece)
            below = f[e, :, (z - 1) * LANES : z * LANES] if z else zero
            above = f[e, :, (z + 1) * LANES : (z + 2) * LANES] if z < NZ - 1 else zero
            g[1, e, :, cols] = (after - before) * 0.5
            g[2, e, :, cols] = (above - below) * 0.5
            lap[e, :, cols] = after + before + above + below - 6.0 * piece

    for copy in avg_copies:
        copy.wait()
    total = avg_mid[...]
    for off in range(1, gx):
        total = total + avg_x[off]
    average = jnp.sum(total, axis=1, keepdims=True) / sample_total
    centred[...] = samples_ref[...] - average

    def pair_low(l, _):
        row = pl.ds(pl.multiple_of(l * HALF, HALF), HALF)
        hi, lo = split(centred[0:HALF, :] * centred[pl.ds(l, 1), :])
        ph[row, :] = hi
        plo[row, :] = lo
        return 0

    def pair_high(l, _):
        row = pl.ds(pl.multiple_of(HALF * HALF + l * K, HALF), K)
        hi, lo = split(centred[...] * centred[pl.ds(l + HALF, 1), :])
        ph[row, :] = hi
        plo[row, :] = lo
        return 0

    lax.fori_loop(0, HALF, pair_low, 0)
    lax.fori_loop(0, HALF, pair_high, 0)
    c_hi, c_lo = split(centred[...])
    c_both = jnp.concatenate([c_hi, c_lo], axis=0)
    for r in range(PAIRS // 256):
        rows = slice(r * 256, (r + 1) * 256)
        first = dot_nt(c_both, ph[rows, :])
        sb[:, rows] = first[0:K] + first[K : 2 * K] + dot_nt(c_hi, plo[rows, :])
    sb[:, PAIRS:WIDE] = jnp.zeros((K, LANES), f32)
    sb[:, PAIRS : PAIRS + K] = dot_nt(centred[...], centred[...], top_degree)

    own_rows = pl.ds(pl.multiple_of(iy * 8, 8), 8)

    def scatter(src, slots, ss, rs):
        copies = []
        for off in range(1, gy):
            target = lax.rem(iy + off, gy)
            rows = pl.ds(pl.multiple_of(target * 8, 8), 8)
            copies.append(send(src.at[rows], slots.at[off], ss.at[off], rs.at[off], "gy", target))
        return copies

    def gather(full, ss, rs):
        return [
            send(
                full.at[own_rows],
                full.at[own_rows],
                ss.at[off],
                rs.at[off],
                "gy",
                lax.rem(iy + off, gy),
            )
            for off in range(1, gy)
        ]

    def finish_scatter(copies, src, slots, out):
        for copy in copies:
            copy.wait()
        summed = src[own_rows, :]
        for off in range(1, gy):
            summed = summed + slots[off]
        out[...] = summed

    def finish_spread(copies, own, slots, full):
        for copy in copies:
            copy.wait()
        summed = own[...]
        for off in range(1, gx):
            summed = summed + slots[off]
        full[own_rows, :] = summed

    copies = scatter(sb, sr1, s_ss, s_rs)
    finish_scatter(copies, sb, sr1, s1)
    copies = spread(s1, sr2, sx_ss, sx_rs, "gx", ix, gx)
    finish_spread(copies, s1, sr2, sfull)
    copies = gather(sfull, sg_ss, sg_rs)
    for copy in copies:
        copy.wait()

    second = sfull[:, PAIRS:WIDE]
    inv = inverse(second)
    folded = dot(inv, sfull[:, 0:PAIRS], top_degree)
    p_k = lax.broadcasted_iota(jnp.int32, (K, PAIRS), 1)
    low = p_k < HALF * HALF
    q = p_k - HALF * HALF
    k_of = jnp.where(low, p_k & (HALF - 1), q & (K - 1))
    l_of = jnp.where(low, p_k >> 4, HALF + (q >> 5))
    row_of = lax.broadcasted_iota(jnp.int32, (K, PAIRS), 0)
    choose = jnp.where(k_of == row_of, 1.0, 0.0).astype(f32)
    spread_cov = dot(second[:, 0:K] / sample_total, choose, top_degree)
    cov_row = jnp.sum(jnp.where(l_of == row_of, spread_cov, 0.0), axis=0, keepdims=True)
    full_coef = jnp.concatenate([folded, jnp.broadcast_to(cov_row, (HALF, PAIRS))], axis=0)
    hi, lo = split(full_coef)
    coef[0:48, :] = hi
    coef[48:96, :] = lo

    for copy in halo:
        copy.wait()
    for e in range(3):
        for z in range(NZ):
            j = e * NZ + z
            cols = slice(z * LANES, (z + 1) * LANES)
            before = xm[pl.ds(j, K, stride=24), :]
            after = xp[pl.ds(j, K, stride=24), :]
            g[0, e, 0:K, cols] = (after - before) * 0.5
            lap[e, 0:K, cols] = lap[e, 0:K, cols] + (after + before)
            before = xm[768 + j : 769 + j, :]
            after = xp[768 + j : 769 + j, :]
            g[0, e, K:ROWS, cols] = jnp.broadcast_to((after - before) * 0.5, (ROWS - K, LANES))
            lap[e, K:ROWS, cols] = lap[e, K:ROWS, cols] + (after + before)

    def advect_low(l, _):
        row = pl.ds(pl.multiple_of(l * HALF, HALF), HALF)
        for e in range(3):
            value = f[0, 0:HALF, :] * g[0, e, pl.ds(l, 1), :]
            for d in range(1, 3):
                value = value + f[d, 0:HALF, :] * g[d, e, pl.ds(l, 1), :]
            hi, lo = split(value)
            bh[e, row, :] = hi
            bl[e, row, :] = lo
        return 0

    def advect_high(i, _):
        l = i + HALF
        base = pl.multiple_of(HALF * HALF + i * K, K)
        row = pl.ds(base, HALF)
        diag = pl.ds(pl.multiple_of(base + HALF, HALF), HALF)
        for e in range(3):
            value = f[0, 0:HALF, :] * g[0, e, pl.ds(l, 1), :]
            value = value + g[0, e, 0:HALF, :] * f[0, pl.ds(l, 1), :]
            other = f[0, HALF:K, :] * g[0, e, pl.ds(l, 1), :]
            for d in range(1, 3):
                value = value + f[d, 0:HALF, :] * g[d, e, pl.ds(l, 1), :]
                value = value + g[d, e, 0:HALF, :] * f[d, pl.ds(l, 1), :]
                other = other + f[d, HALF:K, :] * g[d, e, pl.ds(l, 1), :]
            hi, lo = split(value)
            bh[e, row, :] = hi
            bl[e, row, :] = lo
            hi, lo = split(other)
            bh[e, diag, :] = hi
            bl[e, diag, :] = lo
        return 0

    lax.fori_loop(0, HALF, advect_low, 0)
    lax.fori_loop(0, HALF, advect_high, 0)

    for e in range(3):
        forced = f[0, K : K + 1, :] * g[0, e] + f[0] * g[0, e, K : K + 1, :]
        for d in range(1, 3):
            forced = forced + f[d, K : K + 1, :] * g[d, e] + f[d] * g[d, e, K : K + 1, :]
        lin[e, 0:K] = viscosity * lap[e, 0:K] - forced[0:K]
        lin[e, K:ROWS] = viscosity * lap[e, K:ROWS] - 0.5 * forced[K:ROWS]

    for r in range(PAIRS // 256):
        rows = slice(r * 256, (r + 1) * 256)
        value = jnp.zeros((K, 256), f32)
        for e in range(3):
            first = dot_nt(mt[e], bh[e, rows, :])
            value = value + (first[0:K] + first[K : 2 * K] + dot_nt(mt[e, 0:K], bl[e, rows, :]))
        tb[:, rows] = value
    lin_t = jnp.zeros((K, K), f32)
    lin_n = jnp.zeros((K, K), f32)
    for e in range(3):
        lin_hi, lin_lo = split(lin[e, 0:K, :])
        m_hi, m_lo = mt[e, 0:K], mt[e, K : 2 * K]
        lin_t = lin_t + (dot_nt(m_hi, lin_hi) + dot_nt(m_lo, lin_hi) + dot_nt(m_hi, lin_lo))
        lin_n = lin_n + (dot_nt(lin_hi, m_hi) + dot_nt(lin_hi, m_lo) + dot_nt(lin_lo, m_hi))
    tb[:, PAIRS:WIDE] = jnp.zeros((K, LANES), f32)
    tb[:, PAIRS : PAIRS + K] = lin_t
    tb[:, PAIRS + K : PAIRS + 2 * K] = lin_n

    def tendency(e):
        def step(i, _):
            cols = pl.ds(pl.multiple_of(i * 256, 256), 256)
            first = dot(coef[...], bh[e, :, cols])
            value = first[0:ROWS] + first[48 : 48 + ROWS] + dot(coef[0:48], bl[e, :, cols])[0:ROWS]
            lin[e, :, cols] = lin[e, :, cols] - value
            return 0

        lax.fori_loop(0, CELLS // 256, step, 0)

    copies = scatter(tb, tr1, t_ss, t_rs)
    tendency(0)
    finish_scatter(copies, tb, tr1, t1)
    copies = spread(t1, tr2, tx_ss, tx_rs, "gx", ix, gx)
    tendency(1)
    finish_spread(copies, t1, tr2, tfull)
    copies = gather(tfull, tg_ss, tg_rs)
    tendency(2)
    for e in range(3):
        for z in range(NZ):
            j = e * NZ + z
            mean_out[j : j + 1, :] = lin[e, K : K + 1, z * LANES : (z + 1) * LANES]
    for copy in copies:
        copy.wait()

    triple = tfull[:, 0:PAIRS] / total_cells
    ends = tfull[:, PAIRS:WIDE] / total_cells
    tangent = ends[:, K : 2 * K] - dot_nt(full_coef[0:K], triple, top_degree)
    a_hi, a_lo = split(tangent)
    a_both = jnp.concatenate([a_hi, a_lo], axis=0)
    for e in range(3):
        first = dot(a_both, mt[e, 0:K])
        value = first[0:K] + first[K : 2 * K] + dot(a_hi, mt[e, K : 2 * K])
        value = lin[e, 0:K, :] - value
        for z in range(NZ):
            modes_out[pl.ds(e * NZ + z, K, stride=24), :] = value[:, z * LANES : (z + 1) * LANES]

    offset = jnp.sum(triple * cov_row, axis=1, keepdims=True)
    hi, lo = split(triple)
    t_both = jnp.concatenate([hi, lo], axis=0)
    l_hi, l_lo = split(ends[:, 0:K])
    l_both = jnp.concatenate([l_hi, l_lo], axis=0)
    for i in range(samples_ref.shape[1] // 256):
        cols = slice(i * 256, (i + 1) * 256)
        first = dot(t_both, ph[:, cols])
        value = first[0:K] + first[K : 2 * K] + dot(hi, plo[:, cols])
        s_hi, s_lo = split(centred[:, cols])
        first = dot(l_both, s_hi)
        direct = first[0:K] + first[K : 2 * K] + dot(l_hi, s_lo)
        samples_out[:, cols] = direct - value + offset


def body(mean_field, modes, samples):
    gx, gy = lax.axis_size("gx"), lax.axis_size("gy")
    vmem = pl.BlockSpec(memory_space=pltpu.VMEM)
    count = samples.shape[1]
    dma = lambda n: pltpu.SemaphoreType.DMA((n,))
    scratch = [
        pltpu.VMEM((792, LANES), f32),
        pltpu.VMEM((792, LANES), f32),
        pltpu.VMEM((3, ROWS, CELLS), f32),
        pltpu.VMEM((3, 3, ROWS, CELLS), f32),
        pltpu.VMEM((3, ROWS, CELLS), f32),
        pltpu.VMEM((3, ROWS, CELLS), f32),
        pltpu.VMEM((3, 2 * K, CELLS), bf16),
        pltpu.VMEM((3, PAIRS, CELLS), bf16),
        pltpu.VMEM((3, PAIRS, CELLS), bf16),
        pltpu.VMEM((PAIRS, count), bf16),
        pltpu.VMEM((PAIRS, count), bf16),
        pltpu.VMEM((K, count), f32),
        pltpu.VMEM((96, PAIRS), bf16),
        pltpu.VMEM((K, LANES), f32),
        pltpu.VMEM((gy, K, LANES), f32),
        pltpu.VMEM((K, LANES), f32),
        pltpu.VMEM((gx, K, LANES), f32),
        pltpu.VMEM((2, ROWS, LANES), f32),
        pltpu.VMEM((2, ROWS, LANES), f32),
    ]
    for _ in range(2):
        scratch += [
            pltpu.VMEM((K, WIDE), f32),
            pltpu.VMEM((gy, 8, WIDE), f32),
            pltpu.VMEM((8, WIDE), f32),
            pltpu.VMEM((gx, 8, WIDE), f32),
            pltpu.VMEM((K, WIDE), f32),
        ]
    sems = [dma(6), dma(6), dma(2), dma(2), dma(gy), dma(gy), dma(gx), dma(gx)]
    for _ in range(2):
        sems += [dma(gy), dma(gy), dma(gx), dma(gx), dma(gy), dma(gy)]
    mean_rate, modes_rate, sample_rate = pl.pallas_call(
        functools.partial(kernel, gx, gy),
        out_shape=(
            jax.ShapeDtypeStruct((3 * NZ, LANES), f32),
            jax.ShapeDtypeStruct((K * 3 * NZ, LANES), f32),
            jax.ShapeDtypeStruct(samples.shape, f32),
        ),
        in_specs=[vmem] * 3,
        out_specs=(vmem,) * 3,
        scratch_shapes=scratch + sems,
        compiler_params=pltpu.CompilerParams(
            collective_id=0, has_side_effects=True, vmem_limit_bytes=48 * 1024 * 1024
        ),
    )(mean_field.reshape(3 * NZ, LANES), modes.reshape(K * 3 * NZ, LANES), samples)
    return (mean_rate.reshape(mean_field.shape), modes_rate.reshape(modes.shape), sample_rate)


def solution(mesh):
    placed = (
        P(None, ("groups", "gx"), None, "gy"),
        P(None, None, ("groups", "gx"), None, "gy"),
        P(None, ("groups", "gx", "gy")),
    )
    return jax.shard_map(body, mesh=mesh, in_specs=placed, out_specs=placed, check_vma=False)
```

```python
import functools

import jax
import jax.numpy as jnp
from jax import lax
from jax.experimental import pallas as pl
from jax.experimental.pallas import tpu as pltpu
from jax.sharding import PartitionSpec as P

MESH = pl.DeviceIdType.MESH
top_degree = lax.Precision.HIGHEST
viscosity = 0.2
f32, bf16 = jnp.float32, jnp.bfloat16

K = 32
HALF = 16
NZ = 8
LANES = 128
CELLS = NZ * LANES
PAIRS = HALF * HALF + HALF * K
WIDE = PAIRS + LANES
ROWS = 40


def split(x):
    hi = x.astype(bf16)
    return hi, (x - hi.astype(f32)).astype(bf16)


def dot(a, b, precision=None):
    return lax.dot_general(
        a, b, (((1,), (0,)), ((), ())), precision=precision, preferred_element_type=f32
    )


def dot_nt(a, b, precision=None):
    return lax.dot_general(
        a, b, (((1,), (1,)), ((), ())), precision=precision, preferred_element_type=f32
    )


def inverse(matrix):
    lane = lax.broadcasted_iota(jnp.int32, (K, LANES), 1)
    row = lax.broadcasted_iota(jnp.int32, (K, LANES), 0)
    m = jnp.where(lane < K, matrix, jnp.where(lane == row + K, 1.0, 0.0))
    for k in range(K):
        pivot_row = m[k : k + 1, :] / m[k : k + 1, k : k + 1]
        m = jnp.where(row == k, pivot_row, m - m[:, k : k + 1] * pivot_row)
    return m[:, K : 2 * K]


def kernel(
    gx,
    gy,
    mean_ref,
    modes_ref,
    samples_ref,
    mean_out,
    modes_out,
    samples_out,
    xm,
    xp,
    f,
    g,
    lap,
    lin,
    mt,
    bh,
    bl,
    ph,
    plo,
    centred,
    coef,
    avg_own,
    avg_y,
    avg_mid,
    avg_x,
    edge_send,
    edge_recv,
    sb,
    sr1,
    s1,
    sr2,
    sfull,
    tb,
    tr1,
    t1,
    tr2,
    tfull,
    halo_send,
    halo_recv,
    edge_ss,
    edge_rs,
    ay_ss,
    ay_rs,
    ax_ss,
    ax_rs,
    s_ss,
    s_rs,
    sx_ss,
    sx_rs,
    sg_ss,
    sg_rs,
    t_ss,
    t_rs,
    tx_ss,
    tx_rs,
    tg_ss,
    tg_rs,
):
    ix, iy = lax.axis_index("gx"), lax.axis_index("gy")
    members = gx * gy
    sample_total = samples_ref.shape[1] * members
    total_cells = CELLS * members

    barrier = pltpu.get_barrier_semaphore()
    for off in range(1, gx):
        pl.semaphore_signal(
            barrier, inc=1, device_id={"gx": lax.rem(ix + off, gx)}, device_id_type=MESH
        )
    for off in range(1, gy):
        pl.semaphore_signal(
            barrier, inc=1, device_id={"gy": lax.rem(iy + off, gy)}, device_id_type=MESH
        )
    pl.semaphore_wait(barrier, gx + gy - 2)

    def send(src, dst, ss, rs, axis, target):
        copy = pltpu.make_async_remote_copy(
            src_ref=src,
            dst_ref=dst,
            send_sem=ss,
            recv_sem=rs,
            device_id={axis: target},
            device_id_type=MESH,
        )
        copy.start()
        return copy

    x_next, x_prev = lax.rem(ix + 1, gx), lax.rem(ix + gx - 1, gx)
    y_next, y_prev = lax.rem(iy + 1, gy), lax.rem(iy + gy - 1, gy)

    part = samples_ref[:, 0:LANES]
    for z in range(1, samples_ref.shape[1] // LANES):
        part = part + samples_ref[:, z * LANES : (z + 1) * LANES]
    avg_own[...] = part

    def spread(src, slots, ss, rs, axis, index, count):
        return [
            send(src, slots.at[off], ss.at[off], rs.at[off], axis, lax.rem(index + off, count))
            for off in range(1, count)
        ]

    avg_copies = spread(avg_own, avg_x, ax_ss, ax_rs, "gx", ix, gx)

    halo = []
    halo.append(send(mean_ref, xm.at[768:792], halo_send.at[0], halo_recv.at[0], "gx", x_next))
    halo.append(send(mean_ref, xp.at[768:792], halo_send.at[1], halo_recv.at[1], "gx", x_prev))
    for c in range(4):
        rows = slice(c * 192, (c + 1) * 192)
        for way, (slots, target) in enumerate(((xm, x_next), (xp, x_prev))):
            i = 2 + 2 * c + way
            halo.append(
                send(
                    modes_ref.at[rows], slots.at[rows], halo_send.at[i], halo_recv.at[i], "gx", target
                )
            )

    lane = lax.broadcasted_iota(jnp.int32, (ROWS, LANES), 1)
    to_next = jnp.zeros((ROWS, LANES), f32)
    to_prev = jnp.zeros((ROWS, LANES), f32)
    for e in range(3):
        for z in range(NZ):
            j = e * NZ + z
            cols = slice(z * LANES, (z + 1) * LANES)
            f[e, 0:K, cols] = modes_ref[pl.ds(j, K, stride=24), :]
            f[e, K:ROWS, cols] = jnp.broadcast_to(mean_ref[j : j + 1, :], (ROWS - K, LANES))
            piece = f[e, :, cols]
            to_next = jnp.where(lane == j, pltpu.roll(piece, j + 1, 1), to_next)
            to_prev = jnp.where(lane == j, pltpu.roll(piece, j, 1) if j else piece, to_prev)
    edge_send[0] = to_next
    edge_send[1] = to_prev
    edges = [
        send(edge_send.at[0], edge_recv.at[0], edge_ss.at[0], edge_rs.at[0], "gy", y_next),
        send(edge_send.at[1], edge_recv.at[1], edge_ss.at[1], edge_rs.at[1], "gy", y_prev),
    ]
    for e in range(3):
        hi, lo = split(f[e, 0:K, :])
        mt[e, 0:K, :] = hi
        mt[e, K : 2 * K, :] = lo

    for copy in avg_copies:
        copy.wait()
    total = avg_own[...]
    for off in range(1, gx):
        total = total + avg_x[off]
    avg_mid[...] = total
    avg_copies = spread(avg_mid, avg_y, ay_ss, ay_rs, "gy", iy, gy)

    for copy in edges:
        copy.wait()
    for e in range(3):
        for z in range(NZ):
            j = e * NZ + z
            cols = slice(z * LANES, (z + 1) * LANES)
            piece = f[e, :, cols]
            before = jnp.where(
                lane == 0, pltpu.roll(edge_recv[0], LANES - j, 1) if j else edge_recv[0],
                pltpu.roll(piece, 1, 1),
            )
            after = jnp.where(
                lane == LANES - 1, pltpu.roll(edge_recv[1], LANES - 1 - j, 1),
                pltpu.roll(piece, LANES - 1, 1),
            )
            zero = jnp.zeros_like(piece)
            below = f[e, :, (z - 1) * LANES : z * LANES] if z else zero
            above = f[e, :, (z + 1) * LANES : (z + 2) * LANES] if z < NZ - 1 else zero
            g[1, e, :, cols] = (after - before) * 0.5
            g[2, e, :, cols] = (above - below) * 0.5
            lap[e, :, cols] = after + before + above + below - 6.0 * piece

    for copy in avg_copies:
        copy.wait()
    total = avg_mid[...]
    for off in range(1, gy):
        total = total + avg_y[off]
    average = jnp.sum(total, axis=1, keepdims=True) / sample_total
    centred[...] = samples_ref[...] - average

    def pair_low(l, _):
        row = pl.ds(pl.multiple_of(l * HALF, HALF), HALF)
        hi, lo = split(centred[0:HALF, :] * centred[pl.ds(l, 1), :])
        ph[row, :] = hi
        plo[row, :] = lo
        return 0

    def pair_high(l, _):
        row = pl.ds(pl.multiple_of(HALF * HALF + l * K, HALF), K)
        hi, lo = split(centred[...] * centred[pl.ds(l + HALF, 1), :])
        ph[row, :] = hi
        plo[row, :] = lo
        return 0

    lax.fori_loop(0, HALF, pair_low, 0)
    lax.fori_loop(0, HALF, pair_high, 0)
    c_hi, c_lo = split(centred[...])
    c_both = jnp.concatenate([c_hi, c_lo], axis=0)
    for r in range(PAIRS // 256):
        rows = slice(r * 256, (r + 1) * 256)
        first = dot_nt(c_both, ph[rows, :])
        sb[:, rows] = first[0:K] + first[K : 2 * K] + dot_nt(c_hi, plo[rows, :])
    sb[:, PAIRS:WIDE] = jnp.zeros((K, LANES), f32)
    sb[:, PAIRS : PAIRS + K] = dot_nt(centred[...], centred[...], top_degree)

    own_rows = pl.ds(pl.multiple_of(iy * 8, 8), 8)

    def scatter(src, slots, ss, rs):
        copies = []
        for off in range(1, gy):
            target = lax.rem(iy + off, gy)
            rows = pl.ds(pl.multiple_of(target * 8, 8), 8)
            copies.append(send(src.at[rows], slots.at[off], ss.at[off], rs.at[off], "gy", target))
        return copies

    def gather(full, ss, rs):
        return [
            send(
                full.at[own_rows],
                full.at[own_rows],
                ss.at[off],
                rs.at[off],
                "gy",
                lax.rem(iy + off, gy),
            )
            for off in range(1, gy)
        ]

    def finish_scatter(copies, src, slots, out):
        for copy in copies:
            copy.wait()
        summed = src[own_rows, :]
        for off in range(1, gy):
            summed = summed + slots[off]
        out[...] = summed

    def finish_spread(copies, own, slots, full):
        for copy in copies:
            copy.wait()
        summed = own[...]
        for off in range(1, gx):
            summed = summed + slots[off]
        full[own_rows, :] = summed

    s_copies = scatter(sb, sr1, s_ss, s_rs)

    def slope_x(rows, count, first, stride):
        for e in range(3):
            for z in range(NZ):
                j = e * NZ + z
                cols = slice(z * LANES, (z + 1) * LANES)
                if stride:
                    source = pl.ds(first + j, count, stride=stride)
                else:
                    source = slice(first + j, first + j + 1)
                before = xm[source, :]
                after = xp[source, :]
                g[0, e, rows, cols] = jnp.broadcast_to((after - before) * 0.5, (8, LANES))
                lap[e, rows, cols] = lap[e, rows, cols] + (after + before)

    def force(rows, factor):
        for e in range(3):
            forced = f[0, K : K + 1, :] * g[0, e, rows] + f[0, rows] * g[0, e, K : K + 1, :]
            for d in range(1, 3):
                forced = forced + (
                    f[d, K : K + 1, :] * g[d, e, rows] + f[d, rows] * g[d, e, K : K + 1, :]
                )
            lin[e, rows] = viscosity * lap[e, rows] - factor * forced

    def advect_low(l, _):
        row = pl.ds(pl.multiple_of(l * HALF, HALF), HALF)
        for e in range(3):
            value = f[0, 0:HALF, :] * g[0, e, pl.ds(l, 1), :]
            for d in range(1, 3):
                value = value + f[d, 0:HALF, :] * g[d, e, pl.ds(l, 1), :]
            hi, lo = split(value)
            bh[e, row, :] = hi
            bl[e, row, :] = lo
        return 0

    def advect_high(i, _):
        l = i + HALF
        base = pl.multiple_of(HALF * HALF + i * K, K)
        row = pl.ds(base, HALF)
        diag = pl.ds(pl.multiple_of(base + HALF, HALF), HALF)
        for e in range(3):
            value = f[0, 0:HALF, :] * g[0, e, pl.ds(l, 1), :]
            value = value + g[0, e, 0:HALF, :] * f[0, pl.ds(l, 1), :]
            other = f[0, HALF:K, :] * g[0, e, pl.ds(l, 1), :]
            for d in range(1, 3):
                value = value + f[d, 0:HALF, :] * g[d, e, pl.ds(l, 1), :]
                value = value + g[d, e, 0:HALF, :] * f[d, pl.ds(l, 1), :]
                other = other + f[d, HALF:K, :] * g[d, e, pl.ds(l, 1), :]
            hi, lo = split(value)
            bh[e, row, :] = hi
            bl[e, row, :] = lo
            hi, lo = split(other)
            bh[e, diag, :] = hi
            bl[e, diag, :] = lo
        return 0

    def project(start, count):
        rows = slice(start, start + count)
        value = jnp.zeros((K, count), f32)
        for e in range(3):
            first = dot_nt(mt[e], bh[e, rows, :])
            value = value + (first[0:K] + first[K : 2 * K] + dot_nt(mt[e, 0:K], bl[e, rows, :]))
        tb[:, rows] = value

    halo[0].wait()
    halo[1].wait()
    slope_x(slice(K, ROWS), 1, 768, 0)
    force(slice(K, ROWS), 0.5)
    for c in range(4):
        halo[2 + 2 * c].wait()
        halo[3 + 2 * c].wait()
        rows = slice(8 * c, 8 * c + 8)
        slope_x(rows, 8, 192 * c, 24)
        force(rows, 1.0)
        if c < 2:
            lax.fori_loop(8 * c, 8 * c + 8, advect_low, 0)
        else:
            lax.fori_loop(8 * c - HALF, 8 * c - HALF + 8, advect_high, 0)
        if c == 0:
            finish_scatter(s_copies, sb, sr1, s1)
            s_copies = spread(s1, sr2, sx_ss, sx_rs, "gx", ix, gx)
        if c == 1:
            project(0, 256)
        if c >= 2:
            project(256 * (c - 1), 256)
        if c == 2:
            finish_spread(s_copies, s1, sr2, sfull)
            s_copies = gather(sfull, sg_ss, sg_rs)
    lin_t = jnp.zeros((K, K), f32)
    lin_n = jnp.zeros((K, K), f32)
    for e in range(3):
        lin_hi, lin_lo = split(lin[e, 0:K, :])
        m_hi, m_lo = mt[e, 0:K], mt[e, K : 2 * K]
        lin_t = lin_t + (dot_nt(m_hi, lin_hi) + dot_nt(m_lo, lin_hi) + dot_nt(m_hi, lin_lo))
        lin_n = lin_n + (dot_nt(lin_hi, m_hi) + dot_nt(lin_hi, m_lo) + dot_nt(lin_lo, m_hi))
    tb[:, PAIRS:WIDE] = jnp.zeros((K, LANES), f32)
    tb[:, PAIRS : PAIRS + K] = lin_t
    tb[:, PAIRS + K : PAIRS + 2 * K] = lin_n

    copies = scatter(tb, tr1, t_ss, t_rs)
    for copy in s_copies:
        copy.wait()

    second = sfull[:, PAIRS:WIDE]
    inv = inverse(second)
    folded = dot(inv, sfull[:, 0:PAIRS], top_degree)
    p_k = lax.broadcasted_iota(jnp.int32, (K, PAIRS), 1)
    low = p_k < HALF * HALF
    q = p_k - HALF * HALF
    k_of = jnp.where(low, p_k & (HALF - 1), q & (K - 1))
    l_of = jnp.where(low, p_k >> 4, HALF + (q >> 5))
    row_of = lax.broadcasted_iota(jnp.int32, (K, PAIRS), 0)
    choose = jnp.where(k_of == row_of, 1.0, 0.0).astype(f32)
    spread_cov = dot(second[:, 0:K] / sample_total, choose, top_degree)
    cov_row = jnp.sum(jnp.where(l_of == row_of, spread_cov, 0.0), axis=0, keepdims=True)
    full_coef = jnp.concatenate([folded, jnp.broadcast_to(cov_row, (HALF, PAIRS))], axis=0)
    hi, lo = split(full_coef)
    coef[0:48, :] = hi
    coef[48:96, :] = lo

    def tendency(e):
        def step(i, _):
            cols = pl.ds(pl.multiple_of(i * 256, 256), 256)
            first = dot(coef[...], bh[e, :, cols])
            value = first[0:ROWS] + first[48 : 48 + ROWS] + dot(coef[0:48], bl[e, :, cols])[0:ROWS]
            lin[e, :, cols] = lin[e, :, cols] - value
            return 0

        lax.fori_loop(0, CELLS // 256, step, 0)

    finish_scatter(copies, tb, tr1, t1)
    copies = spread(t1, tr2, tx_ss, tx_rs, "gx", ix, gx)
    tendency(0)
    finish_spread(copies, t1, tr2, tfull)
    copies = gather(tfull, tg_ss, tg_rs)
    tendency(1)
    tendency(2)
    for e in range(3):
        for z in range(NZ):
            j = e * NZ + z
            mean_out[j : j + 1, :] = lin[e, K : K + 1, z * LANES : (z + 1) * LANES]
    for copy in copies:
        copy.wait()

    triple = tfull[:, 0:PAIRS] / total_cells
    ends = tfull[:, PAIRS:WIDE] / total_cells
    tangent = ends[:, K : 2 * K] - dot_nt(full_coef[0:K], triple, top_degree)
    a_hi, a_lo = split(tangent)
    a_both = jnp.concatenate([a_hi, a_lo], axis=0)
    for e in range(3):
        first = dot(a_both, mt[e, 0:K])
        value = first[0:K] + first[K : 2 * K] + dot(a_hi, mt[e, K : 2 * K])
        value = lin[e, 0:K, :] - value
        for z in range(NZ):
            modes_out[pl.ds(e * NZ + z, K, stride=24), :] = value[:, z * LANES : (z + 1) * LANES]

    offset = jnp.sum(triple * cov_row, axis=1, keepdims=True)
    hi, lo = split(triple)
    t_both = jnp.concatenate([hi, lo], axis=0)
    l_hi, l_lo = split(ends[:, 0:K])
    l_both = jnp.concatenate([l_hi, l_lo], axis=0)
    for i in range(samples_ref.shape[1] // 256):
        cols = slice(i * 256, (i + 1) * 256)
        first = dot(t_both, ph[:, cols])
        value = first[0:K] + first[K : 2 * K] + dot(hi, plo[:, cols])
        s_hi, s_lo = split(centred[:, cols])
        first = dot(l_both, s_hi)
        direct = first[0:K] + first[K : 2 * K] + dot(l_hi, s_lo)
        samples_out[:, cols] = direct - value + offset


def body(mean_field, modes, samples):
    gx, gy = lax.axis_size("gx"), lax.axis_size("gy")
    vmem = pl.BlockSpec(memory_space=pltpu.VMEM)
    count = samples.shape[1]
    dma = lambda n: pltpu.SemaphoreType.DMA((n,))
    scratch = [
        pltpu.VMEM((792, LANES), f32),
        pltpu.VMEM((792, LANES), f32),
        pltpu.VMEM((3, ROWS, CELLS), f32),
        pltpu.VMEM((3, 3, ROWS, CELLS), f32),
        pltpu.VMEM((3, ROWS, CELLS), f32),
        pltpu.VMEM((3, ROWS, CELLS), f32),
        pltpu.VMEM((3, 2 * K, CELLS), bf16),
        pltpu.VMEM((3, PAIRS, CELLS), bf16),
        pltpu.VMEM((3, PAIRS, CELLS), bf16),
        pltpu.VMEM((PAIRS, count), bf16),
        pltpu.VMEM((PAIRS, count), bf16),
        pltpu.VMEM((K, count), f32),
        pltpu.VMEM((96, PAIRS), bf16),
        pltpu.VMEM((K, LANES), f32),
        pltpu.VMEM((gy, K, LANES), f32),
        pltpu.VMEM((K, LANES), f32),
        pltpu.VMEM((gx, K, LANES), f32),
        pltpu.VMEM((2, ROWS, LANES), f32),
        pltpu.VMEM((2, ROWS, LANES), f32),
    ]
    for _ in range(2):
        scratch += [
            pltpu.VMEM((K, WIDE), f32),
            pltpu.VMEM((gy, 8, WIDE), f32),
            pltpu.VMEM((8, WIDE), f32),
            pltpu.VMEM((gx, 8, WIDE), f32),
            pltpu.VMEM((K, WIDE), f32),
        ]
    sems = [dma(10), dma(10), dma(2), dma(2), dma(gy), dma(gy), dma(gx), dma(gx)]
    for _ in range(2):
        sems += [dma(gy), dma(gy), dma(gx), dma(gx), dma(gy), dma(gy)]
    mean_rate, modes_rate, sample_rate = pl.pallas_call(
        functools.partial(kernel, gx, gy),
        out_shape=(
            jax.ShapeDtypeStruct((3 * NZ, LANES), f32),
            jax.ShapeDtypeStruct((K * 3 * NZ, LANES), f32),
            jax.ShapeDtypeStruct(samples.shape, f32),
        ),
        in_specs=[vmem] * 3,
        out_specs=(vmem,) * 3,
        scratch_shapes=scratch + sems,
        compiler_params=pltpu.CompilerParams(
            collective_id=0, has_side_effects=True, vmem_limit_bytes=48 * 1024 * 1024
        ),
    )(mean_field.reshape(3 * NZ, LANES), modes.reshape(K * 3 * NZ, LANES), samples)
    return (mean_rate.reshape(mean_field.shape), modes_rate.reshape(modes.shape), sample_rate)


def solution(mesh):
    placed = (
        P(None, ("groups", "gx"), None, "gy"),
        P(None, None, ("groups", "gx"), None, "gy"),
        P(None, ("groups", "gx", "gy")),
    )
    return jax.shard_map(body, mesh=mesh, in_specs=placed, out_specs=placed, check_vma=False)
```

```python
import functools

import jax
import jax.numpy as jnp
from jax import lax
from jax.experimental import pallas as pl
from jax.experimental.pallas import tpu as pltpu
from jax.sharding import PartitionSpec as P

MESH = pl.DeviceIdType.MESH
top_degree = lax.Precision.HIGHEST
viscosity = 0.2
f32, bf16 = jnp.float32, jnp.bfloat16

K = 32
HALF = 16
NZ = 8
LANES = 128
CELLS = NZ * LANES
EARLY = 512
PAIRS = HALF * HALF + HALF * K
WIDE = PAIRS + LANES
LATE = WIDE - EARLY
ROWS = 40


def split(x):
    hi = x.astype(bf16)
    return hi, (x - hi.astype(f32)).astype(bf16)


def dot(a, b, precision=None):
    return lax.dot_general(
        a, b, (((1,), (0,)), ((), ())), precision=precision, preferred_element_type=f32
    )


def dot_nt(a, b, precision=None):
    return lax.dot_general(
        a, b, (((1,), (1,)), ((), ())), precision=precision, preferred_element_type=f32
    )


def inverse(matrix):
    lane = lax.broadcasted_iota(jnp.int32, (K, LANES), 1)
    row = lax.broadcasted_iota(jnp.int32, (K, LANES), 0)
    m = jnp.where(lane < K, matrix, jnp.where(lane == row + K, 1.0, 0.0))
    for k in range(K):
        pivot_row = m[k : k + 1, :] / m[k : k + 1, k : k + 1]
        m = jnp.where(row == k, pivot_row, m - m[:, k : k + 1] * pivot_row)
    return m[:, K : 2 * K]


def kernel(
    gx,
    gy,
    mean_ref,
    modes_ref,
    samples_ref,
    mean_out,
    modes_out,
    samples_out,
    xm,
    xp,
    f,
    g,
    lap,
    lin,
    mt,
    bh,
    bl,
    ph,
    plo,
    centred,
    coef,
    avg_own,
    avg_y,
    avg_mid,
    avg_x,
    edge_send,
    edge_recv,
    sb,
    sr1,
    s1,
    sr2,
    sfull,
    ub,
    ur1,
    u1,
    ur2,
    ufull,
    tb,
    tr1,
    t1,
    tr2,
    tfull,
    halo_send,
    halo_recv,
    edge_ss,
    edge_rs,
    ay_ss,
    ay_rs,
    ax_ss,
    ax_rs,
    s_ss,
    s_rs,
    sx_ss,
    sx_rs,
    sg_ss,
    sg_rs,
    u_ss,
    u_rs,
    ux_ss,
    ux_rs,
    ug_ss,
    ug_rs,
    t_ss,
    t_rs,
    tx_ss,
    tx_rs,
    tg_ss,
    tg_rs,
):
    ix, iy = lax.axis_index("gx"), lax.axis_index("gy")
    members = gx * gy
    sample_total = samples_ref.shape[1] * members
    total_cells = CELLS * members

    barrier = pltpu.get_barrier_semaphore()
    for off in range(1, gx):
        pl.semaphore_signal(
            barrier, inc=1, device_id={"gx": lax.rem(ix + off, gx)}, device_id_type=MESH
        )
    for off in range(1, gy):
        pl.semaphore_signal(
            barrier, inc=1, device_id={"gy": lax.rem(iy + off, gy)}, device_id_type=MESH
        )
    pl.semaphore_wait(barrier, gx + gy - 2)

    def send(src, dst, ss, rs, axis, target):
        copy = pltpu.make_async_remote_copy(
            src_ref=src,
            dst_ref=dst,
            send_sem=ss,
            recv_sem=rs,
            device_id={axis: target},
            device_id_type=MESH,
        )
        copy.start()
        return copy

    x_next, x_prev = lax.rem(ix + 1, gx), lax.rem(ix + gx - 1, gx)
    y_next, y_prev = lax.rem(iy + 1, gy), lax.rem(iy + gy - 1, gy)

    part = samples_ref[:, 0:LANES]
    for z in range(1, samples_ref.shape[1] // LANES):
        part = part + samples_ref[:, z * LANES : (z + 1) * LANES]
    avg_own[...] = part

    def spread(src, slots, ss, rs, axis, index, count):
        return [
            send(src, slots.at[off], ss.at[off], rs.at[off], axis, lax.rem(index + off, count))
            for off in range(1, count)
        ]

    avg_copies = spread(avg_own, avg_x, ax_ss, ax_rs, "gx", ix, gx)

    halo = []
    halo.append(send(mean_ref, xm.at[768:792], halo_send.at[0], halo_recv.at[0], "gx", x_next))
    halo.append(send(mean_ref, xp.at[768:792], halo_send.at[1], halo_recv.at[1], "gx", x_prev))

    def send_chunk(c):
        rows = slice(c * 192, (c + 1) * 192)
        if c >= 2:
            halo[2 * c - 2].wait_send()
            halo[2 * c - 1].wait_send()
        for way, (slots, target) in enumerate(((xm, x_next), (xp, x_prev))):
            i = 2 + 2 * c + way
            halo.append(
                send(
                    modes_ref.at[rows], slots.at[rows], halo_send.at[i], halo_recv.at[i], "gx", target
                )
            )

    send_chunk(0)
    send_chunk(1)

    lane = lax.broadcasted_iota(jnp.int32, (ROWS, LANES), 1)
    to_next = jnp.zeros((ROWS, LANES), f32)
    to_prev = jnp.zeros((ROWS, LANES), f32)
    for e in range(3):
        for z in range(NZ):
            j = e * NZ + z
            cols = slice(z * LANES, (z + 1) * LANES)
            f[e, 0:K, cols] = modes_ref[pl.ds(j, K, stride=24), :]
            f[e, K:ROWS, cols] = jnp.broadcast_to(mean_ref[j : j + 1, :], (ROWS - K, LANES))
            piece = f[e, :, cols]
            to_next = jnp.where(lane == j, pltpu.roll(piece, j + 1, 1), to_next)
            to_prev = jnp.where(lane == j, pltpu.roll(piece, j, 1) if j else piece, to_prev)
    edge_send[0] = to_next
    edge_send[1] = to_prev
    edges = [
        send(edge_send.at[0], edge_recv.at[0], edge_ss.at[0], edge_rs.at[0], "gy", y_next),
        send(edge_send.at[1], edge_recv.at[1], edge_ss.at[1], edge_rs.at[1], "gy", y_prev),
    ]
    for e in range(3):
        hi, lo = split(f[e, 0:K, :])
        mt[e, 0:K, :] = hi
        mt[e, K : 2 * K, :] = lo

    for copy in avg_copies:
        copy.wait()
    total = avg_own[...]
    for off in range(1, gx):
        total = total + avg_x[off]
    avg_mid[...] = total
    avg_copies = spread(avg_mid, avg_y, ay_ss, ay_rs, "gy", iy, gy)

    for copy in edges:
        copy.wait()
    for e in range(3):
        for z in range(NZ):
            j = e * NZ + z
            cols = slice(z * LANES, (z + 1) * LANES)
            piece = f[e, :, cols]
            before = jnp.where(
                lane == 0, pltpu.roll(edge_recv[0], LANES - j, 1) if j else edge_recv[0],
                pltpu.roll(piece, 1, 1),
            )
            after = jnp.where(
                lane == LANES - 1, pltpu.roll(edge_recv[1], LANES - 1 - j, 1),
                pltpu.roll(piece, LANES - 1, 1),
            )
            zero = jnp.zeros_like(piece)
            below = f[e, :, (z - 1) * LANES : z * LANES] if z else zero
            above = f[e, :, (z + 1) * LANES : (z + 2) * LANES] if z < NZ - 1 else zero
            g[1, e, :, cols] = (after - before) * 0.5
            g[2, e, :, cols] = (above - below) * 0.5
            lap[e, :, cols] = after + before + above + below - 6.0 * piece

    def slope_x(rows, count, first, stride):
        for e in range(3):
            for z in range(NZ):
                j = e * NZ + z
                cols = slice(z * LANES, (z + 1) * LANES)
                if stride:
                    source = pl.ds(first + j, count, stride=stride)
                else:
                    source = slice(first + j, first + j + 1)
                before = xm[source, :]
                after = xp[source, :]
                g[0, e, rows, cols] = jnp.broadcast_to((after - before) * 0.5, (8, LANES))
                lap[e, rows, cols] = lap[e, rows, cols] + (after + before)

    def force(rows, factor):
        for e in range(3):
            forced = f[0, K : K + 1, :] * g[0, e, rows] + f[0, rows] * g[0, e, K : K + 1, :]
            for d in range(1, 3):
                forced = forced + (
                    f[d, K : K + 1, :] * g[d, e, rows] + f[d, rows] * g[d, e, K : K + 1, :]
                )
            lin[e, rows] = viscosity * lap[e, rows] - factor * forced

    def advect_low(l, _):
        row = pl.ds(pl.multiple_of(l * HALF, HALF), HALF)
        for e in range(3):
            value = f[0, 0:HALF, :] * g[0, e, pl.ds(l, 1), :]
            for d in range(1, 3):
                value = value + f[d, 0:HALF, :] * g[d, e, pl.ds(l, 1), :]
            hi, lo = split(value)
            bh[e, row, :] = hi
            bl[e, row, :] = lo
        return 0

    def advect_high(i, _):
        l = i + HALF
        base = pl.multiple_of(HALF * HALF + i * K, K)
        row = pl.ds(base, HALF)
        diag = pl.ds(pl.multiple_of(base + HALF, HALF), HALF)
        for e in range(3):
            value = f[0, 0:HALF, :] * g[0, e, pl.ds(l, 1), :]
            value = value + g[0, e, 0:HALF, :] * f[0, pl.ds(l, 1), :]
            other = f[0, HALF:K, :] * g[0, e, pl.ds(l, 1), :]
            for d in range(1, 3):
                value = value + f[d, 0:HALF, :] * g[d, e, pl.ds(l, 1), :]
                value = value + g[d, e, 0:HALF, :] * f[d, pl.ds(l, 1), :]
                other = other + f[d, HALF:K, :] * g[d, e, pl.ds(l, 1), :]
            hi, lo = split(value)
            bh[e, row, :] = hi
            bl[e, row, :] = lo
            hi, lo = split(other)
            bh[e, diag, :] = hi
            bl[e, diag, :] = lo
        return 0

    def project(start, count):
        rows = slice(start, start + count)
        first = jnp.zeros((count, 2 * K), f32)
        second = jnp.zeros((count, K), f32)
        for e in range(3):
            first = first + dot_nt(bh[e, rows, :], mt[e])
            second = second + dot_nt(bl[e, rows, :], mt[e, 0:K])
        first = first.T
        value = first[0:K] + first[K : 2 * K] + second.T
        if start < EARLY:
            ub[:, rows] = value
        else:
            tb[:, start - EARLY : start - EARLY + count] = value

    def work(c):
        halo[2 + 2 * c].wait_recv()
        halo[3 + 2 * c].wait_recv()
        rows = slice(8 * c, 8 * c + 8)
        slope_x(rows, 8, 192 * c, 24)
        force(rows, 1.0)
        if c < 2:
            lax.fori_loop(8 * c, 8 * c + 8, advect_low, 0)
        else:
            lax.fori_loop(8 * c - HALF, 8 * c - HALF + 8, advect_high, 0)

    send_chunk(2)
    halo[0].wait()
    halo[1].wait()
    slope_x(slice(K, ROWS), 1, 768, 0)
    force(slice(K, ROWS), 0.5)
    work(0)

    for copy in avg_copies:
        copy.wait()
    total = avg_mid[...]
    for off in range(1, gy):
        total = total + avg_y[off]
    average = jnp.sum(total, axis=1, keepdims=True) / sample_total
    centred[...] = samples_ref[...] - average

    def pair_low(l, _):
        row = pl.ds(pl.multiple_of(l * HALF, HALF), HALF)
        hi, lo = split(centred[0:HALF, :] * centred[pl.ds(l, 1), :])
        ph[row, :] = hi
        plo[row, :] = lo
        return 0

    def pair_high(l, _):
        row = pl.ds(pl.multiple_of(HALF * HALF + l * K, HALF), K)
        hi, lo = split(centred[...] * centred[pl.ds(l + HALF, 1), :])
        ph[row, :] = hi
        plo[row, :] = lo
        return 0

    lax.fori_loop(0, HALF, pair_low, 0)
    lax.fori_loop(0, HALF, pair_high, 0)
    c_hi, c_lo = split(centred[...])
    c_both = jnp.concatenate([c_hi, c_lo], axis=0)
    for r in range(PAIRS // 256):
        rows = slice(r * 256, (r + 1) * 256)
        first = dot_nt(c_both, ph[rows, :])
        sb[:, rows] = first[0:K] + first[K : 2 * K] + dot_nt(c_hi, plo[rows, :])
    sb[:, PAIRS:WIDE] = jnp.zeros((K, LANES), f32)
    sb[:, PAIRS : PAIRS + K] = dot_nt(centred[...], centred[...], top_degree)

    own_rows = pl.ds(pl.multiple_of(iy * 8, 8), 8)

    def scatter(src, slots, ss, rs):
        copies = []
        for off in range(1, gy):
            target = lax.rem(iy + off, gy)
            rows = pl.ds(pl.multiple_of(target * 8, 8), 8)
            copies.append(send(src.at[rows], slots.at[off], ss.at[off], rs.at[off], "gy", target))
        return copies

    def gather(full, ss, rs):
        return [
            send(
                full.at[own_rows],
                full.at[own_rows],
                ss.at[off],
                rs.at[off],
                "gy",
                lax.rem(iy + off, gy),
            )
            for off in range(1, gy)
        ]

    def finish_scatter(copies, src, slots, out):
        for copy in copies:
            copy.wait()
        summed = src[own_rows, :]
        for off in range(1, gy):
            summed = summed + slots[off]
        out[...] = summed

    def finish_spread(copies, own, slots, full):
        for copy in copies:
            copy.wait()
        summed = own[...]
        for off in range(1, gx):
            summed = summed + slots[off]
        full[own_rows, :] = summed

    s_copies = scatter(sb, sr1, s_ss, s_rs)

    send_chunk(3)
    work(1)
    project(0, 256)
    finish_scatter(s_copies, sb, sr1, s1)
    s_copies = spread(s1, sr2, sx_ss, sx_rs, "gx", ix, gx)
    work(2)
    project(256, 256)
    u_copies = scatter(ub, ur1, u_ss, u_rs)
    finish_spread(s_copies, s1, sr2, sfull)
    s_copies = gather(sfull, sg_ss, sg_rs)
    work(3)
    finish_scatter(u_copies, ub, ur1, u1)
    u_copies = spread(u1, ur2, ux_ss, ux_rs, "gx", ix, gx)
    project(512, 256)
    halo[8].wait_send()
    halo[9].wait_send()
    halo[6].wait_send()
    halo[7].wait_send()
    lin_t = jnp.zeros((K, K), f32)
    lin_n = jnp.zeros((K, K), f32)
    for e in range(3):
        lin_hi, lin_lo = split(lin[e, 0:K, :])
        m_hi, m_lo = mt[e, 0:K], mt[e, K : 2 * K]
        lin_t = lin_t + (dot_nt(m_hi, lin_hi) + dot_nt(m_lo, lin_hi) + dot_nt(m_hi, lin_lo))
        lin_n = lin_n + (dot_nt(lin_hi, m_hi) + dot_nt(lin_hi, m_lo) + dot_nt(lin_lo, m_hi))
    tb[:, PAIRS - EARLY : LATE] = jnp.zeros((K, LANES), f32)
    ends_at = PAIRS - EARLY
    tb[:, ends_at : ends_at + K] = lin_t
    tb[:, ends_at + K : ends_at + 2 * K] = lin_n

    copies = scatter(tb, tr1, t_ss, t_rs)
    finish_spread(u_copies, u1, ur2, ufull)
    u_copies = gather(ufull, ug_ss, ug_rs)
    finish_scatter(copies, tb, tr1, t1)
    copies = spread(t1, tr2, tx_ss, tx_rs, "gx", ix, gx)
    for copy in s_copies:
        copy.wait()

    second = sfull[:, PAIRS:WIDE]
    inv = inverse(second)
    folded = dot(inv, sfull[:, 0:PAIRS], top_degree)
    p_k = lax.broadcasted_iota(jnp.int32, (K, PAIRS), 1)
    low = p_k < HALF * HALF
    q = p_k - HALF * HALF
    k_of = jnp.where(low, p_k & (HALF - 1), q & (K - 1))
    l_of = jnp.where(low, p_k >> 4, HALF + (q >> 5))
    row_of = lax.broadcasted_iota(jnp.int32, (K, PAIRS), 0)
    choose = jnp.where(k_of == row_of, 1.0, 0.0).astype(f32)
    spread_cov = dot(second[:, 0:K] / sample_total, choose, top_degree)
    cov_row = jnp.sum(jnp.where(l_of == row_of, spread_cov, 0.0), axis=0, keepdims=True)
    full_coef = jnp.concatenate([folded, jnp.broadcast_to(cov_row, (HALF, PAIRS))], axis=0)
    hi, lo = split(full_coef)
    coef[0:48, :] = hi
    coef[48:96, :] = lo

    def tendency(e):
        def step(i, _):
            cols = pl.ds(pl.multiple_of(i * 256, 256), 256)
            first = dot(coef[...], bh[e, :, cols])
            value = first[0:ROWS] + first[48 : 48 + ROWS] + dot(coef[0:48], bl[e, :, cols])[0:ROWS]
            lin[e, :, cols] = lin[e, :, cols] - value
            return 0

        lax.fori_loop(0, CELLS // 256, step, 0)

    tendency(0)
    finish_spread(copies, t1, tr2, tfull)
    copies = gather(tfull, tg_ss, tg_rs)
    tendency(1)
    tendency(2)
    for e in range(3):
        for z in range(NZ):
            j = e * NZ + z
            mean_out[j : j + 1, :] = lin[e, K : K + 1, z * LANES : (z + 1) * LANES]
    for copy in copies:
        copy.wait()

    for copy in u_copies:
        copy.wait()
    triple = jnp.concatenate([ufull[...], tfull[:, 0:ends_at]], axis=1) / total_cells
    ends = tfull[:, ends_at:LATE] / total_cells
    tangent = ends[:, K : 2 * K] - dot_nt(full_coef[0:K], triple, top_degree)
    a_hi, a_lo = split(tangent)
    a_both = jnp.concatenate([a_hi, a_lo], axis=0)
    for e in range(3):
        first = dot(a_both, mt[e, 0:K])
        value = first[0:K] + first[K : 2 * K] + dot(a_hi, mt[e, K : 2 * K])
        value = lin[e, 0:K, :] - value
        for z in range(NZ):
            modes_out[pl.ds(e * NZ + z, K, stride=24), :] = value[:, z * LANES : (z + 1) * LANES]

    offset = jnp.sum(triple * cov_row, axis=1, keepdims=True)
    hi, lo = split(triple)
    t_both = jnp.concatenate([hi, lo], axis=0)
    l_hi, l_lo = split(ends[:, 0:K])
    l_both = jnp.concatenate([l_hi, l_lo], axis=0)
    for i in range(samples_ref.shape[1] // 256):
        cols = slice(i * 256, (i + 1) * 256)
        first = dot(t_both, ph[:, cols])
        value = first[0:K] + first[K : 2 * K] + dot(hi, plo[:, cols])
        s_hi, s_lo = split(centred[:, cols])
        first = dot(l_both, s_hi)
        direct = first[0:K] + first[K : 2 * K] + dot(l_hi, s_lo)
        samples_out[:, cols] = direct - value + offset


def body(mean_field, modes, samples):
    gx, gy = lax.axis_size("gx"), lax.axis_size("gy")
    vmem = pl.BlockSpec(memory_space=pltpu.VMEM)
    count = samples.shape[1]
    dma = lambda n: pltpu.SemaphoreType.DMA((n,))
    scratch = [
        pltpu.VMEM((792, LANES), f32),
        pltpu.VMEM((792, LANES), f32),
        pltpu.VMEM((3, ROWS, CELLS), f32),
        pltpu.VMEM((3, 3, ROWS, CELLS), f32),
        pltpu.VMEM((3, ROWS, CELLS), f32),
        pltpu.VMEM((3, ROWS, CELLS), f32),
        pltpu.VMEM((3, 2 * K, CELLS), bf16),
        pltpu.VMEM((3, PAIRS, CELLS), bf16),
        pltpu.VMEM((3, PAIRS, CELLS), bf16),
        pltpu.VMEM((PAIRS, count), bf16),
        pltpu.VMEM((PAIRS, count), bf16),
        pltpu.VMEM((K, count), f32),
        pltpu.VMEM((96, PAIRS), bf16),
        pltpu.VMEM((K, LANES), f32),
        pltpu.VMEM((gy, K, LANES), f32),
        pltpu.VMEM((K, LANES), f32),
        pltpu.VMEM((gx, K, LANES), f32),
        pltpu.VMEM((2, ROWS, LANES), f32),
        pltpu.VMEM((2, ROWS, LANES), f32),
    ]
    for width in (WIDE, EARLY, LATE):
        scratch += [
            pltpu.VMEM((K, width), f32),
            pltpu.VMEM((gy, 8, width), f32),
            pltpu.VMEM((8, width), f32),
            pltpu.VMEM((gx, 8, width), f32),
            pltpu.VMEM((K, width), f32),
        ]
    sems = [dma(10), dma(10), dma(2), dma(2), dma(gy), dma(gy), dma(gx), dma(gx)]
    for _ in range(3):
        sems += [dma(gy), dma(gy), dma(gx), dma(gx), dma(gy), dma(gy)]
    mean_rate, modes_rate, sample_rate = pl.pallas_call(
        functools.partial(kernel, gx, gy),
        out_shape=(
            jax.ShapeDtypeStruct((3 * NZ, LANES), f32),
            jax.ShapeDtypeStruct((K * 3 * NZ, LANES), f32),
            jax.ShapeDtypeStruct(samples.shape, f32),
        ),
        in_specs=[vmem] * 3,
        out_specs=(vmem,) * 3,
        scratch_shapes=scratch + sems,
        compiler_params=pltpu.CompilerParams(
            collective_id=0, has_side_effects=True, vmem_limit_bytes=48 * 1024 * 1024
        ),
    )(mean_field.reshape(3 * NZ, LANES), modes.reshape(K * 3 * NZ, LANES), samples)
    return (mean_rate.reshape(mean_field.shape), modes_rate.reshape(modes.shape), sample_rate)


def solution(mesh):
    placed = (
        P(None, ("groups", "gx"), None, "gy"),
        P(None, None, ("groups", "gx"), None, "gy"),
        P(None, ("groups", "gx", "gy")),
    )
    return jax.shard_map(body, mesh=mesh, in_specs=placed, out_specs=placed, check_vma=False)
```

```python
import functools

import jax
import jax.numpy as jnp
from jax import lax
from jax.experimental import pallas as pl
from jax.experimental.pallas import tpu as pltpu
from jax.sharding import PartitionSpec as P

MESH = pl.DeviceIdType.MESH
top_degree = lax.Precision.HIGHEST
viscosity = 0.2
f32, bf16 = jnp.float32, jnp.bfloat16

K = 32
HALF = 16
NZ = 8
LANES = 128
CELLS = NZ * LANES
EARLY = 512
PAIRS = HALF * HALF + HALF * K
WIDE = PAIRS + LANES
LATE = WIDE - EARLY
ROWS = 40


def split(x):
    hi = x.astype(bf16)
    return hi, (x - hi.astype(f32)).astype(bf16)


def dot(a, b, precision=None):
    return lax.dot_general(
        a, b, (((1,), (0,)), ((), ())), precision=precision, preferred_element_type=f32
    )


def dot_nt(a, b, precision=None):
    return lax.dot_general(
        a, b, (((1,), (1,)), ((), ())), precision=precision, preferred_element_type=f32
    )


def inverse(matrix):
    lane = lax.broadcasted_iota(jnp.int32, (K, LANES), 1)
    row = lax.broadcasted_iota(jnp.int32, (K, LANES), 0)
    m = jnp.where(lane < K, matrix, jnp.where(lane == row + K, 1.0, 0.0))
    for k in range(K):
        pivot_row = m[k : k + 1, :] / m[k : k + 1, k : k + 1]
        m = jnp.where(row == k, pivot_row, m - m[:, k : k + 1] * pivot_row)
    return m[:, K : 2 * K]


def kernel(
    gx,
    gy,
    mean_ref,
    modes_ref,
    samples_ref,
    mean_out,
    modes_out,
    samples_out,
    xm,
    xp,
    f,
    g,
    lap,
    lin,
    mt,
    bh,
    bl,
    ph,
    plo,
    centred,
    coef,
    avg_own,
    avg_y,
    avg_mid,
    avg_x,
    edge_send,
    edge_recv,
    sb,
    sr1,
    s1,
    sr2,
    sfull,
    ub,
    ur1,
    u1,
    ur2,
    ufull,
    tb,
    tr1,
    t1,
    tr2,
    tfull,
    halo_send,
    halo_recv,
    edge_ss,
    edge_rs,
    ay_ss,
    ay_rs,
    ax_ss,
    ax_rs,
    s_ss,
    s_rs,
    sx_ss,
    sx_rs,
    sg_ss,
    sg_rs,
    u_ss,
    u_rs,
    ux_ss,
    ux_rs,
    ug_ss,
    ug_rs,
    t_ss,
    t_rs,
    tx_ss,
    tx_rs,
    tg_ss,
    tg_rs,
):
    ix, iy = lax.axis_index("gx"), lax.axis_index("gy")
    members = gx * gy
    sample_total = samples_ref.shape[1] * members
    total_cells = CELLS * members

    barrier = pltpu.get_barrier_semaphore()
    for off in range(1, gx):
        pl.semaphore_signal(
            barrier, inc=1, device_id={"gx": lax.rem(ix + off, gx)}, device_id_type=MESH
        )
    for off in range(1, gy):
        pl.semaphore_signal(
            barrier, inc=1, device_id={"gy": lax.rem(iy + off, gy)}, device_id_type=MESH
        )
    pl.semaphore_wait(barrier, gx + gy - 2)

    def send(src, dst, ss, rs, axis, target):
        copy = pltpu.make_async_remote_copy(
            src_ref=src,
            dst_ref=dst,
            send_sem=ss,
            recv_sem=rs,
            device_id={axis: target},
            device_id_type=MESH,
        )
        copy.start()
        return copy

    x_next, x_prev = lax.rem(ix + 1, gx), lax.rem(ix + gx - 1, gx)
    y_next, y_prev = lax.rem(iy + 1, gy), lax.rem(iy + gy - 1, gy)

    part = samples_ref[:, 0:LANES]
    for z in range(1, samples_ref.shape[1] // LANES):
        part = part + samples_ref[:, z * LANES : (z + 1) * LANES]
    avg_own[...] = part

    def spread(src, slots, ss, rs, axis, index, count):
        return [
            send(src, slots.at[off], ss.at[off], rs.at[off], axis, lax.rem(index + off, count))
            for off in range(1, count)
        ]

    avg_copies = spread(avg_own, avg_x, ax_ss, ax_rs, "gx", ix, gx)

    halo = []
    halo.append(send(mean_ref, xm.at[768:792], halo_send.at[0], halo_recv.at[0], "gx", x_next))
    halo.append(send(mean_ref, xp.at[768:792], halo_send.at[1], halo_recv.at[1], "gx", x_prev))

    def send_chunk(c):
        rows = slice(c * 192, (c + 1) * 192)
        for way, (slots, target) in enumerate(((xm, x_next), (xp, x_prev))):
            i = 2 + 2 * c + way
            halo.append(
                send(
                    modes_ref.at[rows], slots.at[rows], halo_send.at[i], halo_recv.at[i], "gx", target
                )
            )

    for c in range(4):
        send_chunk(c)

    lane = lax.broadcasted_iota(jnp.int32, (ROWS, LANES), 1)
    to_next = jnp.zeros((ROWS, LANES), f32)
    to_prev = jnp.zeros((ROWS, LANES), f32)
    for e in range(3):
        for z in range(NZ):
            j = e * NZ + z
            cols = slice(z * LANES, (z + 1) * LANES)
            f[e, 0:K, cols] = modes_ref[pl.ds(j, K, stride=24), :]
            f[e, K:ROWS, cols] = jnp.broadcast_to(mean_ref[j : j + 1, :], (ROWS - K, LANES))
            piece = f[e, :, cols]
            to_next = jnp.where(lane == j, pltpu.roll(piece, j + 1, 1), to_next)
            to_prev = jnp.where(lane == j, pltpu.roll(piece, j, 1) if j else piece, to_prev)
    edge_send[0] = to_next
    edge_send[1] = to_prev
    edges = [
        send(edge_send.at[0], edge_recv.at[0], edge_ss.at[0], edge_rs.at[0], "gy", y_next),
        send(edge_send.at[1], edge_recv.at[1], edge_ss.at[1], edge_rs.at[1], "gy", y_prev),
    ]
    for e in range(3):
        hi, lo = split(f[e, 0:K, :])
        mt[e, 0:K, :] = hi
        mt[e, K : 2 * K, :] = lo

    for copy in avg_copies:
        copy.wait()
    total = avg_own[...]
    for off in range(1, gx):
        total = total + avg_x[off]
    avg_mid[...] = total
    avg_copies = spread(avg_mid, avg_y, ay_ss, ay_rs, "gy", iy, gy)

    for copy in edges:
        copy.wait()
    for e in range(3):
        for z in range(NZ):
            j = e * NZ + z
            cols = slice(z * LANES, (z + 1) * LANES)
            piece = f[e, :, cols]
            before = jnp.where(
                lane == 0, pltpu.roll(edge_recv[0], LANES - j, 1) if j else edge_recv[0],
                pltpu.roll(piece, 1, 1),
            )
            after = jnp.where(
                lane == LANES - 1, pltpu.roll(edge_recv[1], LANES - 1 - j, 1),
                pltpu.roll(piece, LANES - 1, 1),
            )
            zero = jnp.zeros_like(piece)
            below = f[e, :, (z - 1) * LANES : z * LANES] if z else zero
            above = f[e, :, (z + 1) * LANES : (z + 2) * LANES] if z < NZ - 1 else zero
            g[1, e, :, cols] = (after - before) * 0.5
            g[2, e, :, cols] = (above - below) * 0.5
            lap[e, :, cols] = after + before + above + below - 6.0 * piece

    def slope_x(rows, count, first, stride):
        for e in range(3):
            for z in range(NZ):
                j = e * NZ + z
                cols = slice(z * LANES, (z + 1) * LANES)
                if stride:
                    source = pl.ds(first + j, count, stride=stride)
                else:
                    source = slice(first + j, first + j + 1)
                before = xm[source, :]
                after = xp[source, :]
                g[0, e, rows, cols] = jnp.broadcast_to((after - before) * 0.5, (8, LANES))
                lap[e, rows, cols] = lap[e, rows, cols] + (after + before)

    def force(rows, factor):
        for e in range(3):
            forced = f[0, K : K + 1, :] * g[0, e, rows] + f[0, rows] * g[0, e, K : K + 1, :]
            for d in range(1, 3):
                forced = forced + (
                    f[d, K : K + 1, :] * g[d, e, rows] + f[d, rows] * g[d, e, K : K + 1, :]
                )
            lin[e, rows] = viscosity * lap[e, rows] - factor * forced

    def advect_low(l, _):
        row = pl.ds(pl.multiple_of(l * HALF, HALF), HALF)
        for e in range(3):
            value = f[0, 0:HALF, :] * g[0, e, pl.ds(l, 1), :]
            for d in range(1, 3):
                value = value + f[d, 0:HALF, :] * g[d, e, pl.ds(l, 1), :]
            hi, lo = split(value)
            bh[e, row, :] = hi
            bl[e, row, :] = lo
        return 0

    def advect_high(i, _):
        l = i + HALF
        base = pl.multiple_of(HALF * HALF + i * K, K)
        row = pl.ds(base, HALF)
        diag = pl.ds(pl.multiple_of(base + HALF, HALF), HALF)
        for e in range(3):
            value = f[0, 0:HALF, :] * g[0, e, pl.ds(l, 1), :]
            value = value + g[0, e, 0:HALF, :] * f[0, pl.ds(l, 1), :]
            other = f[0, HALF:K, :] * g[0, e, pl.ds(l, 1), :]
            for d in range(1, 3):
                value = value + f[d, 0:HALF, :] * g[d, e, pl.ds(l, 1), :]
                value = value + g[d, e, 0:HALF, :] * f[d, pl.ds(l, 1), :]
                other = other + f[d, HALF:K, :] * g[d, e, pl.ds(l, 1), :]
            hi, lo = split(value)
            bh[e, row, :] = hi
            bl[e, row, :] = lo
            hi, lo = split(other)
            bh[e, diag, :] = hi
            bl[e, diag, :] = lo
        return 0

    def project(start, count):
        rows = slice(start, start + count)
        first = jnp.zeros((count, 2 * K), f32)
        second = jnp.zeros((count, K), f32)
        for e in range(3):
            first = first + dot_nt(bh[e, rows, :], mt[e])
            second = second + dot_nt(bl[e, rows, :], mt[e, 0:K])
        first = first.T
        value = first[0:K] + first[K : 2 * K] + second.T
        if start < EARLY:
            ub[:, rows] = value
        else:
            tb[:, start - EARLY : start - EARLY + count] = value

    def work(c):
        halo[2 + 2 * c].wait_recv()
        halo[3 + 2 * c].wait_recv()
        rows = slice(8 * c, 8 * c + 8)
        slope_x(rows, 8, 192 * c, 24)
        force(rows, 1.0)
        if c < 2:
            lax.fori_loop(8 * c, 8 * c + 8, advect_low, 0)
        else:
            lax.fori_loop(8 * c - HALF, 8 * c - HALF + 8, advect_high, 0)

    halo[0].wait()
    halo[1].wait()
    slope_x(slice(K, ROWS), 1, 768, 0)
    force(slice(K, ROWS), 0.5)
    work(0)

    for copy in avg_copies:
        copy.wait()
    total = avg_mid[...]
    for off in range(1, gy):
        total = total + avg_y[off]
    average = jnp.sum(total, axis=1, keepdims=True) / sample_total
    centred[...] = samples_ref[...] - average

    def pair_low(l, _):
        row = pl.ds(pl.multiple_of(l * HALF, HALF), HALF)
        hi, lo = split(centred[0:HALF, :] * centred[pl.ds(l, 1), :])
        ph[row, :] = hi
        plo[row, :] = lo
        return 0

    def pair_high(l, _):
        row = pl.ds(pl.multiple_of(HALF * HALF + l * K, HALF), K)
        hi, lo = split(centred[...] * centred[pl.ds(l + HALF, 1), :])
        ph[row, :] = hi
        plo[row, :] = lo
        return 0

    lax.fori_loop(0, HALF, pair_low, 0)
    lax.fori_loop(0, HALF, pair_high, 0)
    c_hi, c_lo = split(centred[...])
    c_both = jnp.concatenate([c_hi, c_lo], axis=0)
    for r in range(PAIRS // 256):
        rows = slice(r * 256, (r + 1) * 256)
        first = dot_nt(c_both, ph[rows, :])
        sb[:, rows] = first[0:K] + first[K : 2 * K] + dot_nt(c_hi, plo[rows, :])
    sb[:, PAIRS:WIDE] = jnp.zeros((K, LANES), f32)
    sb[:, PAIRS : PAIRS + K] = dot_nt(centred[...], centred[...], top_degree)

    own_rows = pl.ds(pl.multiple_of(iy * 8, 8), 8)

    def scatter(src, slots, ss, rs):
        copies = []
        for off in range(1, gy):
            target = lax.rem(iy + off, gy)
            rows = pl.ds(pl.multiple_of(target * 8, 8), 8)
            copies.append(send(src.at[rows], slots.at[off], ss.at[off], rs.at[off], "gy", target))
        return copies

    def gather(full, ss, rs):
        return [
            send(
                full.at[own_rows],
                full.at[own_rows],
                ss.at[off],
                rs.at[off],
                "gy",
                lax.rem(iy + off, gy),
            )
            for off in range(1, gy)
        ]

    def finish_scatter(copies, src, slots, out):
        for copy in copies:
            copy.wait()
        summed = src[own_rows, :]
        for off in range(1, gy):
            summed = summed + slots[off]
        out[...] = summed

    def finish_spread(copies, own, slots, full):
        for copy in copies:
            copy.wait()
        summed = own[...]
        for off in range(1, gx):
            summed = summed + slots[off]
        full[own_rows, :] = summed

    s_copies = scatter(sb, sr1, s_ss, s_rs)

    work(1)
    project(0, 256)
    finish_scatter(s_copies, sb, sr1, s1)
    s_copies = spread(s1, sr2, sx_ss, sx_rs, "gx", ix, gx)
    work(2)
    project(256, 256)
    u_copies = scatter(ub, ur1, u_ss, u_rs)
    finish_spread(s_copies, s1, sr2, sfull)
    s_copies = gather(sfull, sg_ss, sg_rs)
    work(3)
    finish_scatter(u_copies, ub, ur1, u1)
    u_copies = spread(u1, ur2, ux_ss, ux_rs, "gx", ix, gx)
    project(512, 256)
    for copy in halo[2:]:
        copy.wait_send()
    lin_t = jnp.zeros((K, K), f32)
    lin_n = jnp.zeros((K, K), f32)
    for e in range(3):
        lin_hi, lin_lo = split(lin[e, 0:K, :])
        m_hi, m_lo = mt[e, 0:K], mt[e, K : 2 * K]
        lin_t = lin_t + (dot_nt(m_hi, lin_hi) + dot_nt(m_lo, lin_hi) + dot_nt(m_hi, lin_lo))
        lin_n = lin_n + (dot_nt(lin_hi, m_hi) + dot_nt(lin_hi, m_lo) + dot_nt(lin_lo, m_hi))
    tb[:, PAIRS - EARLY : LATE] = jnp.zeros((K, LANES), f32)
    ends_at = PAIRS - EARLY
    tb[:, ends_at : ends_at + K] = lin_t
    tb[:, ends_at + K : ends_at + 2 * K] = lin_n

    copies = scatter(tb, tr1, t_ss, t_rs)
    finish_spread(u_copies, u1, ur2, ufull)
    u_copies = gather(ufull, ug_ss, ug_rs)
    finish_scatter(copies, tb, tr1, t1)
    copies = spread(t1, tr2, tx_ss, tx_rs, "gx", ix, gx)
    for copy in s_copies:
        copy.wait()

    second = sfull[:, PAIRS:WIDE]
    inv = inverse(second)
    folded = dot(inv, sfull[:, 0:PAIRS], top_degree)
    p_k = lax.broadcasted_iota(jnp.int32, (K, PAIRS), 1)
    low = p_k < HALF * HALF
    q = p_k - HALF * HALF
    k_of = jnp.where(low, p_k & (HALF - 1), q & (K - 1))
    l_of = jnp.where(low, p_k >> 4, HALF + (q >> 5))
    row_of = lax.broadcasted_iota(jnp.int32, (K, PAIRS), 0)
    choose = jnp.where(k_of == row_of, 1.0, 0.0).astype(f32)
    spread_cov = dot(second[:, 0:K] / sample_total, choose, top_degree)
    cov_row = jnp.sum(jnp.where(l_of == row_of, spread_cov, 0.0), axis=0, keepdims=True)
    full_coef = jnp.concatenate([folded, jnp.broadcast_to(cov_row, (HALF, PAIRS))], axis=0)
    hi, lo = split(full_coef)
    coef[0:48, :] = hi
    coef[48:96, :] = lo

    def tendency(e):
        def step(i, _):
            cols = pl.ds(pl.multiple_of(i * 256, 256), 256)
            first = dot(coef[...], bh[e, :, cols])
            value = first[0:ROWS] + first[48 : 48 + ROWS] + dot(coef[0:48], bl[e, :, cols])[0:ROWS]
            lin[e, :, cols] = lin[e, :, cols] - value
            return 0

        lax.fori_loop(0, CELLS // 256, step, 0)

    tendency(0)
    finish_spread(copies, t1, tr2, tfull)
    copies = gather(tfull, tg_ss, tg_rs)
    tendency(1)
    tendency(2)
    for e in range(3):
        for z in range(NZ):
            j = e * NZ + z
            mean_out[j : j + 1, :] = lin[e, K : K + 1, z * LANES : (z + 1) * LANES]
    for copy in copies:
        copy.wait()

    for copy in u_copies:
        copy.wait()
    triple = jnp.concatenate([ufull[...], tfull[:, 0:ends_at]], axis=1) / total_cells
    ends = tfull[:, ends_at:LATE] / total_cells
    tangent = ends[:, K : 2 * K] - dot_nt(full_coef[0:K], triple, top_degree)
    a_hi, a_lo = split(tangent)
    a_both = jnp.concatenate([a_hi, a_lo], axis=0)
    for e in range(3):
        first = dot(a_both, mt[e, 0:K])
        value = first[0:K] + first[K : 2 * K] + dot(a_hi, mt[e, K : 2 * K])
        value = lin[e, 0:K, :] - value
        for z in range(NZ):
            modes_out[pl.ds(e * NZ + z, K, stride=24), :] = value[:, z * LANES : (z + 1) * LANES]

    offset = jnp.sum(triple * cov_row, axis=1, keepdims=True)
    hi, lo = split(triple)
    t_both = jnp.concatenate([hi, lo], axis=0)
    l_hi, l_lo = split(ends[:, 0:K])
    l_both = jnp.concatenate([l_hi, l_lo], axis=0)
    for i in range(samples_ref.shape[1] // 256):
        cols = slice(i * 256, (i + 1) * 256)
        first = dot(t_both, ph[:, cols])
        value = first[0:K] + first[K : 2 * K] + dot(hi, plo[:, cols])
        s_hi, s_lo = split(centred[:, cols])
        first = dot(l_both, s_hi)
        direct = first[0:K] + first[K : 2 * K] + dot(l_hi, s_lo)
        samples_out[:, cols] = direct - value + offset


def body(mean_field, modes, samples):
    gx, gy = lax.axis_size("gx"), lax.axis_size("gy")
    vmem = pl.BlockSpec(memory_space=pltpu.VMEM)
    count = samples.shape[1]
    dma = lambda n: pltpu.SemaphoreType.DMA((n,))
    scratch = [
        pltpu.VMEM((792, LANES), f32),
        pltpu.VMEM((792, LANES), f32),
        pltpu.VMEM((3, ROWS, CELLS), f32),
        pltpu.VMEM((3, 3, ROWS, CELLS), f32),
        pltpu.VMEM((3, ROWS, CELLS), f32),
        pltpu.VMEM((3, ROWS, CELLS), f32),
        pltpu.VMEM((3, 2 * K, CELLS), bf16),
        pltpu.VMEM((3, PAIRS, CELLS), bf16),
        pltpu.VMEM((3, PAIRS, CELLS), bf16),
        pltpu.VMEM((PAIRS, count), bf16),
        pltpu.VMEM((PAIRS, count), bf16),
        pltpu.VMEM((K, count), f32),
        pltpu.VMEM((96, PAIRS), bf16),
        pltpu.VMEM((K, LANES), f32),
        pltpu.VMEM((gy, K, LANES), f32),
        pltpu.VMEM((K, LANES), f32),
        pltpu.VMEM((gx, K, LANES), f32),
        pltpu.VMEM((2, ROWS, LANES), f32),
        pltpu.VMEM((2, ROWS, LANES), f32),
    ]
    for width in (WIDE, EARLY, LATE):
        scratch += [
            pltpu.VMEM((K, width), f32),
            pltpu.VMEM((gy, 8, width), f32),
            pltpu.VMEM((8, width), f32),
            pltpu.VMEM((gx, 8, width), f32),
            pltpu.VMEM((K, width), f32),
        ]
    sems = [dma(10), dma(10), dma(2), dma(2), dma(gy), dma(gy), dma(gx), dma(gx)]
    for _ in range(3):
        sems += [dma(gy), dma(gy), dma(gx), dma(gx), dma(gy), dma(gy)]
    mean_rate, modes_rate, sample_rate = pl.pallas_call(
        functools.partial(kernel, gx, gy),
        out_shape=(
            jax.ShapeDtypeStruct((3 * NZ, LANES), f32),
            jax.ShapeDtypeStruct((K * 3 * NZ, LANES), f32),
            jax.ShapeDtypeStruct(samples.shape, f32),
        ),
        in_specs=[vmem] * 3,
        out_specs=(vmem,) * 3,
        scratch_shapes=scratch + sems,
        compiler_params=pltpu.CompilerParams(
            collective_id=0, has_side_effects=True, vmem_limit_bytes=48 * 1024 * 1024
        ),
    )(mean_field.reshape(3 * NZ, LANES), modes.reshape(K * 3 * NZ, LANES), samples)
    return (mean_rate.reshape(mean_field.shape), modes_rate.reshape(modes.shape), sample_rate)


def solution(mesh):
    placed = (
        P(None, ("groups", "gx"), None, "gy"),
        P(None, None, ("groups", "gx"), None, "gy"),
        P(None, ("groups", "gx", "gy")),
    )
    return jax.shard_map(body, mesh=mesh, in_specs=placed, out_specs=placed, check_vma=False)
```
